512 devices in a mesh: seq: 32 (over z, core), blk: 16 (over x, y).
Axes of the slice: x: 4, y: 4, z: 16, core: 2. Of those that a mesh axis runs over, the one named last changes fastest.
Arguments:
- query: bfloat16 [65536, 4096], P(('seq', 'blk')), may hold values from -12 to 12
- key: bfloat16 [65536, 4096], P(('seq', 'blk')), may hold values from -80 to 80
- value: bfloat16 [65536, 4096], P(('seq', 'blk')), may hold values from -6 to 6
- recompute_index: int32 [3072], P(('seq', 'blk')), may hold values from 0 to 127, as said below
- counts: int32 [512], P(('seq', 'blk')), may hold values from 1 to 6, as said below
- timestep: int32 [1], replicated, may hold values from 0 to 49
- gate_table: float32 [50, 4096], replicated, may hold values from 0.5 to 2
Outputs:
- gated: bfloat16 [3072, 4096], P(('seq', 'blk'))
The draws below stay inside these ranges and needn't reach their ends.
Inputs may be any that keep to these rules, and one draw needn't show every extreme that they name: `recompute_index`: the 6 positions of one device are distinct. `counts`: some device has all 6 slots live.
All inputs are finite; a program needn't handle non-finite values.
Results may differ from the reference program's by a relative error of at most 0.012.
Values may be sent and summed in bfloat16 or wider, within the bound.
No kernel may reach another device: no remote copies, remote signals or barrier semaphores. Data moves between devices by JAX's collectives and lax.ppermute only.
A program may use at most 64 MiB of HBM per device.

```python
import math
import jax
import jax.numpy as jnp
from jax import lax

HD = 128
HEADS = 32
TOK_DEV = 128
RMAX = 6
STEPS = 50
HW = 4096
TOKENS = 65536
N_SEQ = 32
N_BLK = 16


def slot_rows(subkey):
    return jax.random.permutation(subkey, TOK_DEV)[:RMAX]


def recompute_slots(key):
    devices = TOKENS // TOK_DEV
    subkeys = jax.random.split(jax.random.fold_in(key, 11), devices)
    return jax.vmap(slot_rows)(subkeys).astype(jnp.int32)


def query_values(key):
    drawn = 2.0 * jax.random.normal(jax.random.fold_in(key, 21), (TOKENS, HEADS * HD), jnp.float32)
    return jnp.clip(drawn, -12.0, 12.0)


def draw_recompute_index(key, part):
    return recompute_slots(key).reshape(-1)


def draw_counts(key, part):
    devices = TOKENS // TOK_DEV
    live = jax.random.randint(jax.random.fold_in(key, 12), (devices,), 1, RMAX + 1)
    fullest = jax.random.randint(jax.random.fold_in(key, 13), (), 0, devices)
    return jnp.where(jnp.arange(devices) == fullest, RMAX, live).astype(jnp.int32)


def draw_query(key, part):
    values = query_values(key)
    return values.astype(jnp.bfloat16)


def draw_key(key, part):
    drawn = 2.0 * jax.random.normal(jax.random.fold_in(key, 22), (TOKENS, HEADS * HD), jnp.float32)
    base = jnp.clip(drawn, -12.0, 12.0)
    return base.astype(jnp.bfloat16)


def level_of(key, shape, cuts, smallest, largest):
    loudness, own = 1.0, jax.random.fold_in(key, 6)
    for dim, blocks in cuts:
        heights = jnp.exp(jax.random.uniform(jax.random.fold_in(own, dim), (blocks,), jnp.float32, smallest / len(cuts), largest / len(cuts)))
        loudness = loudness * jnp.repeat(heights, shape[dim] // blocks).reshape([-1 if axis == dim else 1 for axis in range(len(shape))])
    return loudness


def bell_draw(stream_key, dims, scale, limit, pieces=(), kind=jnp.bfloat16):
    entries = scale * jax.random.normal(stream_key, dims, jnp.float32)
    if pieces:
        entries = entries * level_of(stream_key, dims, pieces, -0.22, 0.18)
    return jnp.clip(entries, -limit, limit).astype(kind)


def setup_inputs(seed: int = 0) -> dict:
    seeds = jax.random.split(jax.random.key(seed), 8)
    query = draw_query(jax.random.fold_in(seeds[7], 71), 0)
    key = draw_key(jax.random.fold_in(seeds[7], 71), 0)
    value = bell_draw(seeds[2], (TOKENS, HW), 1.0, 6.0, ((0, 512),))
    recompute_index = draw_recompute_index(jax.random.fold_in(seeds[7], 71), 0)
    counts = draw_counts(jax.random.fold_in(seeds[7], 71), 0)
    timestep = jax.random.randint(seeds[5], (1,), 0, STEPS).astype(jnp.int32)
    gate_table = jnp.clip(jax.random.uniform(seeds[6], (STEPS, HW), jnp.float32, 0.5, 2.0), 0.5, 2.0)
    return dict(query=query, key=key, value=value, recompute_index=recompute_index, counts=counts, timestep=timestep, gate_table=gate_table)


def block_part(rows_head, keys_block, values_block):
    scale = 1.0 / math.sqrt(HD)
    scores = jnp.dot(rows_head.astype(jnp.float32), keys_block.astype(jnp.float32).T) * scale
    top = lax.optimization_barrier(jnp.max(scores, axis=1))
    powers = jnp.exp(scores - top[:, None])
    total = lax.optimization_barrier(jnp.sum(powers, axis=1))
    weights = powers.astype(jnp.bfloat16).astype(jnp.float32)
    mixed = jnp.dot(weights, values_block.astype(jnp.float32)) / total[:, None]
    return (mixed.astype(jnp.bfloat16), top, total)

def combine_parts(mixed, top, total):
    peak = lax.optimization_barrier(jnp.max(top, axis=0))
    factor = total * jnp.exp(top - peak)
    summed = lax.optimization_barrier(jnp.sum(factor[..., None] * mixed.astype(jnp.float32), axis=0))
    return (summed / lax.optimization_barrier(jnp.sum(factor, axis=0))[..., None]).astype(jnp.bfloat16)

def reference(query, key, value, recompute_index, counts, timestep, gate_table):
    devices = N_SEQ * N_BLK
    slot_table = recompute_index.reshape(devices, RMAX)
    token = (jnp.arange(devices, dtype=jnp.int32)[:, None] * TOK_DEV + slot_table).reshape(-1)
    rows = query[token].reshape(-1, HEADS, HD)
    key_five = key.reshape(N_SEQ, N_BLK, TOK_DEV, HEADS, HD)
    value_five = value.reshape(N_SEQ, N_BLK, TOK_DEV, HEADS, HD)

    def one_head(head):
        rows_head = lax.dynamic_index_in_dim(rows, head, 1, keepdims=False)
        keys_head = lax.dynamic_index_in_dim(key_five, head, 3, keepdims=False)
        keys_head = keys_head.transpose(1, 0, 2, 3).reshape(N_BLK, N_SEQ * TOK_DEV, HD)
        values_head = lax.dynamic_index_in_dim(value_five, head, 3, keepdims=False)
        values_head = values_head.transpose(1, 0, 2, 3).reshape(N_BLK, N_SEQ * TOK_DEV, HD)

        def one_block(pair):
            return block_part(rows_head, pair[0], pair[1])
        mixed, top, total = lax.map(one_block, (keys_head, values_head))
        return combine_parts(mixed, top, total)
    attention = lax.map(one_head, jnp.arange(HEADS, dtype=jnp.int32))
    attention = attention.transpose(1, 0, 2).reshape(-1, HEADS * HD)
    gate = lax.dynamic_index_in_dim(gate_table, timestep[0], 0, keepdims=False)
    gated = (gate[None, :] * attention.astype(jnp.float32)).astype(jnp.bfloat16)
    live = (jnp.arange(RMAX, dtype=jnp.int32)[None, :] < counts[:, None]).reshape(-1)
    return jnp.where(live[:, None], gated, jnp.zeros_like(gated))
```

```python
import functools
import math

import jax
import jax.numpy as jnp
from jax import lax
from jax.experimental import pallas as pl
from jax.experimental.pallas import tpu as pltpu
from jax.sharding import Mesh, PartitionSpec as P

HD = 128
HEADS = 32
TOK = 128
SLOTS = 6
PAD = 8
CHIPS_Z = 16
NZO = 8
ROWS = HEADS * SLOTS
TAIL = 16
MSG = ROWS + TAIL
SCALE = math.log2(math.e) / math.sqrt(HD)
KEYS = HEADS * TOK
CHUNK = 1024
BF = jnp.bfloat16
F32 = jnp.float32
NT = (((1,), (1,)), ((), ()))
PLANE = ("c", "blk")
VMEM = pl.BlockSpec(memory_space=pltpu.VMEM)
SMEM = pl.BlockSpec(memory_space=pltpu.SMEM)


def iota(shape, dim):
    return lax.broadcasted_iota(jnp.int32, shape, dim)


def choose_body(index_ref, count_ref, query_ref, out_ref):
    row = iota((16, TOK), 0)
    col = iota((16, TOK), 1)
    hot = jnp.zeros((16, TOK), F32)
    for r in range(SLOTS):
        hot = jnp.where((row == r) & (col == index_ref[r]), 1.0, hot)
    rows = jnp.dot(hot.astype(BF), query_ref[...], preferred_element_type=F32)
    count = count_ref[0].astype(F32)
    place = iota((PAD, HD), 0)
    for h in range(HEADS):
        part = rows[:PAD, h * HD:(h + 1) * HD]
        out_ref[h] = jnp.where(place == SLOTS, count, part).astype(BF)


def choose(query, index, counts):
    return pl.pallas_call(
        choose_body,
        out_shape=jax.ShapeDtypeStruct((HEADS, PAD, HD), BF),
        in_specs=[SMEM, SMEM, VMEM],
        out_specs=VMEM,
        name="choose",
    )(index, counts, query)


def split_body(per, key_ref, value_ref, out_ref):
    for h in range(per):
        out_ref[h, :TOK, :] = key_ref[:, h * HD:(h + 1) * HD]
        out_ref[h, TOK:, :] = value_ref[:, h * HD:(h + 1) * HD]


def split_heads(key, value):
    per = 8
    return pl.pallas_call(
        functools.partial(split_body, per),
        grid=(HEADS // per,),
        in_specs=[pl.BlockSpec((TOK, per * HD), lambda i: (0, i))] * 2,
        out_specs=pl.BlockSpec((per, 2 * TOK, HD), lambda i: (i, 0, 0)),
        out_shape=jax.ShapeDtypeStruct((HEADS, 2 * TOK, HD), BF),
        name="split_heads",
    )(key, value)


def compact_body(rows_ref, out_ref, back_ref):
    n = HEADS * PAD
    rows = rows_ref[...].astype(F32).reshape(n, HD).astype(BF)
    down, across = iota((n, n), 0), iota((n, n), 1)
    pick = jnp.where(across == (down // PAD) * PAD + SLOTS, 1.0, 0.0).astype(BF)
    count_col = jnp.dot(pick, rows, preferred_element_type=F32)
    slot_col = iota((n, HD), 0) % PAD
    live_col = (slot_col.astype(F32) < count_col) & (slot_col < SLOTS)
    live_col = jnp.where(live_col, 1.0, 0.0)
    below = jnp.where(across < down, 1.0, 0.0).astype(BF)
    pos_col = jnp.dot(below, live_col.astype(BF), preferred_element_type=F32)
    pos_col = jnp.concatenate([pos_col, pos_col], 1)
    live_two = jnp.concatenate([live_col, live_col], 1)
    back_ref[...] = jnp.where(pos_col == across.astype(F32), live_two, 0.0).astype(BF)
    first = jnp.where(iota((16, HD), 1) == 0, 1.0, 0.0).astype(BF)
    live_row = lax.dot_general(first, live_col.astype(BF), NT, preferred_element_type=F32)
    above = jnp.where(down < across, 1.0, 0.0).astype(BF)
    pos_row = jnp.dot(live_row.astype(BF), above, preferred_element_type=F32)
    pos_row = jnp.broadcast_to(pos_row[:1], (n, n))
    live_row = jnp.broadcast_to(live_row[:1], (n, n))
    move = jnp.where(pos_row == down.astype(F32), live_row, 0.0).astype(BF)
    moved = jnp.dot(move, rows, preferred_element_type=F32)
    out_ref[:ROWS] = moved[:ROWS].astype(BF)
    total = jnp.sum(live_col, axis=0, keepdims=True)
    out_ref[ROWS:] = jnp.broadcast_to(total, (TAIL, HD)).astype(BF)


def compact(rows):
    n = HEADS * PAD
    return pl.pallas_call(
        compact_body,
        out_shape=(jax.ShapeDtypeStruct((MSG, HD), BF), jax.ShapeDtypeStruct((n, n), BF)),
        in_specs=[VMEM],
        out_specs=(VMEM, VMEM),
        name="compact",
    )(rows)


def tail_of(first, second):
    place = iota((TAIL, HD), 0)
    tile = jnp.zeros((TAIL, HD), F32)
    for half, lanes in enumerate((first, second)):
        rest = lanes
        for term in range(3):
            piece = rest.astype(BF).astype(F32)
            rest = rest - piece
            tile = jnp.where(place == 2 * term + half, piece, tile)
    return tile.astype(BF)


def lanes_of(tail):
    tail = tail.astype(F32)
    return tail[0:2] + tail[2:4] + tail[4:6]


def column_to_lanes(column):
    n = column.shape[0]
    full = jnp.broadcast_to(column, (n, HD))
    out = []
    for at in (0, HD):
        size = min(HD, n - at)
        if size <= 0:
            out.append(jnp.zeros((1, HD), F32))
            continue
        diag = iota((size, HD), 0) == iota((size, HD), 1)
        out.append(jnp.sum(jnp.where(diag, full[at:at + size], 0.0), axis=0, keepdims=True))
    return out


def lanes_to_column(lanes):
    out = []
    for half, size in enumerate((HD, ROWS - HD)):
        diag = iota((size, HD), 0) == iota((size, HD), 1)
        full = jnp.broadcast_to(lanes[half:half + 1], (size, HD))
        out.append(jnp.sum(jnp.where(diag, full, 0.0), axis=1, keepdims=True))
    return jnp.concatenate(out, 0)


def attend_rows(group, rows, query_ref, kv_ref, out_ref):
    size = group * rows
    query = query_ref[:, 0, :rows, :].reshape(size, HD)
    per = CHUNK // TOK
    top = mixed = total = None
    for j in range(KEYS // CHUNK):
        keys = kv_ref[j * per:(j + 1) * per, :TOK, :].reshape(CHUNK, HD)
        values = kv_ref[j * per:(j + 1) * per, TOK:, :].reshape(CHUNK, HD)
        scores = lax.dot_general(query, keys, NT, preferred_element_type=F32)
        high = scores[:, :HD]
        for t in range(1, per):
            high = jnp.maximum(high, scores[:, t * HD:(t + 1) * HD])
        high = jnp.broadcast_to(jnp.max(high, axis=1, keepdims=True) * SCALE, (size, HD))
        peak = high if top is None else jnp.maximum(top, high)
        weights, part_total = [], None
        for t in range(per):
            power = jnp.exp2(scores[:, t * HD:(t + 1) * HD] * SCALE - peak)
            part_total = power if part_total is None else part_total + power
            weights.append(power.astype(BF))
        part = jnp.dot(jnp.concatenate(weights, 1), values, preferred_element_type=F32)
        if top is None:
            mixed, total = part, part_total
        else:
            fade = jnp.exp2(top - peak)
            mixed = mixed * fade + part
            total = total * fade + part_total
        top = peak
    total = jnp.sum(total, axis=1, keepdims=True)
    out_ref[:, :rows, :] = (mixed / total).astype(BF).reshape(group, rows, HD)
    level = top[:, :1] + jnp.log2(total)
    for g in range(group):
        out_ref[g, ROWS:, :] = tail_of(*column_to_lanes(level[g * rows:(g + 1) * rows]))


def attend_body(group, side_ref, query_ref, kv_ref, out_ref):
    attend_rows(group, ROWS, query_ref, kv_ref, out_ref)


def attend(side, query, kv):
    group = 2
    work = NZO * ROWS * KEYS * HD * 4
    return pl.pallas_call(
        functools.partial(attend_body, group),
        grid_spec=pltpu.PrefetchScalarGridSpec(
            num_scalar_prefetch=1,
            grid=(NZO // group,),
            in_specs=[
                pl.BlockSpec((group, 1, MSG, HD), lambda i, side: (i, side[0], 0, 0)),
                pl.BlockSpec((HEADS, 2 * TOK, HD), lambda i, side: (0, 0, 0)),
            ],
            out_specs=pl.BlockSpec((group, MSG, HD), lambda i, side: (i, 0, 0)),
        ),
        out_shape=jax.ShapeDtypeStruct((NZO, MSG, HD), BF),
        compiler_params=pltpu.CompilerParams(vmem_limit_bytes=40 * 2**20),
        cost_estimate=pl.CostEstimate(
            flops=2 * work, bytes_accessed=6 * 2**20, transcendentals=NZO * ROWS * KEYS
        ),
        name="attend",
    )(side, query, kv)


def pair_body(group, own_ref, other_ref, out_ref):
    for g in range(group):
        a, b = lanes_of(own_ref[g, ROWS:, :]), lanes_of(other_ref[g, ROWS:, :])
        peak = jnp.maximum(a, b)
        wa, wb = jnp.exp2(a - peak), jnp.exp2(b - peak)
        both = wa + wb
        level = peak + jnp.log2(both)
        ca, cb = lanes_to_column(wa / both), lanes_to_column(wb / both)
        out_ref[g, :ROWS, :] = (
            own_ref[g, :ROWS, :].astype(F32) * ca + other_ref[g, :ROWS, :].astype(F32) * cb
        ).astype(BF)
        out_ref[g, ROWS:, :] = tail_of(level[0:1], level[1:2])


def merge_pair(own, other):
    group = 4
    spec = pl.BlockSpec((group, MSG, HD), lambda i: (i, 0, 0))
    return pl.pallas_call(
        functools.partial(pair_body, group),
        grid=(NZO // group,),
        in_specs=[spec, spec],
        out_specs=spec,
        out_shape=jax.ShapeDtypeStruct((NZO, MSG, HD), BF),
        name="merge_pair",
    )(own, other)


def finish_body(parts_ref, live_ref, back_ref, out_ref):
    levels = [lanes_of(parts_ref[i, ROWS:, :]) for i in range(NZO)]
    peak = functools.reduce(jnp.maximum, levels)
    weights = [jnp.exp2(level - peak) for level in levels]
    both = functools.reduce(jnp.add, weights)
    mixed = None
    for i in range(NZO):
        column = lanes_to_column(weights[i] / both)
        part = parts_ref[i, :ROWS, :].astype(F32) * column
        mixed = part if mixed is None else mixed + part
    count = live_ref[ROWS:, :].astype(F32)[:1]
    alive = iota((ROWS, HD), 0).astype(F32) < count
    mixed = jnp.where(alive, mixed, 0.0).astype(BF)
    rows = jnp.dot(back_ref[:, :ROWS], mixed, preferred_element_type=F32)
    out_ref[...] = rows.reshape(HEADS, PAD, HD).astype(BF)


def finish(parts, live, back):
    return pl.pallas_call(
        finish_body,
        out_shape=jax.ShapeDtypeStruct((HEADS, PAD, HD), BF),
        in_specs=[VMEM, VMEM, VMEM],
        out_specs=VMEM,
        name="finish",
    )(parts, live, back)


def gate_body(count_ref, rows_ref, gate_ref, out_ref):
    alive = iota((PAD, HD), 0) < count_ref[0]
    for h in range(HEADS):
        gated = gate_ref[:, h * HD:(h + 1) * HD] * rows_ref[h].astype(F32)
        gated = jnp.where(alive, gated, 0.0)
        out_ref[:, h * HD:(h + 1) * HD] = gated[:SLOTS].astype(BF)


def apply_gate(counts, rows, gate):
    return pl.pallas_call(
        gate_body,
        out_shape=jax.ShapeDtypeStruct((SLOTS, HEADS * HD), BF),
        in_specs=[SMEM, VMEM, VMEM],
        out_specs=VMEM,
        name="apply_gate",
    )(counts, rows, gate)


def after(value, token):
    return lax.optimization_barrier((value, token))[0]


def swap(x, axes):
    return lax.all_to_all(x, axes, split_axis=0, concat_axis=0, tiled=True)


def local(query, key, value, index, counts, timestep, gate_table):
    side = lax.axis_index("zi").astype(jnp.int32).reshape(1)
    mine = choose(query, index, counts)
    kv = split_heads(key, value)
    plane_rows = swap(mine, PLANE)
    kv = swap(after(kv, plane_rows), PLANE)
    live, back = compact(plane_rows)
    rows = lax.all_gather(live, ("zo", "zi"), axis=0, tiled=False)
    rows = rows.reshape(NZO, 2, MSG, HD)
    away = attend(1 - side, rows, kv)
    arrived = lax.ppermute(away, "zi", [(0, 1), (1, 0)])
    own = attend(side, rows, kv)
    merged = merge_pair(own, arrived)
    parts = swap(merged, "zo")
    sent = finish(parts, live, back)
    heads = swap(sent, PLANE)
    gate = lax.dynamic_slice_in_dim(gate_table, timestep[0], 1, 0)
    return apply_gate(counts, heads, gate)


def solution(mesh):
    blk = mesh.shape["blk"]
    inner = Mesh(mesh.devices.reshape(NZO, 2, 2, blk), ("zo", "zi", "c", "blk"))
    every = ("zo", "zi", "c", "blk")
    in_specs = (
        P(every, None),
        P(every, None),
        P(every, None),
        P(every),
        P(every),
        P(),
        P(),
    )
    return jax.shard_map(
        local, mesh=inner, in_specs=in_specs, out_specs=P(every, None), check_vma=False
    )
```

```python
import functools
import math

import jax
import jax.numpy as jnp
from jax import lax
from jax.experimental import pallas as pl
from jax.experimental.pallas import tpu as pltpu
from jax.sharding import Mesh, PartitionSpec as P

HD = 128
HEADS = 32
TOK = 128
SLOTS = 6
PAD = 8
CHIPS_Z = 16
NZO = 8
ROWS = HEADS * SLOTS
TAIL = 16
MSG = ROWS + TAIL
TIERS = (128, 144, ROWS)
SCALE = math.log2(math.e) / math.sqrt(HD)
KEYS = HEADS * TOK
CHUNK = 1024
BF = jnp.bfloat16
F32 = jnp.float32
NT = (((1,), (1,)), ((), ()))
PLANE = ("c", "blk")
SMALL = pltpu.CompilerParams(vmem_limit_bytes=12 * 2**20)
VMEM = pl.BlockSpec(memory_space=pltpu.VMEM)
SMEM = pl.BlockSpec(memory_space=pltpu.SMEM)


def iota(shape, dim):
    return lax.broadcasted_iota(jnp.int32, shape, dim)


def choose_body(index_ref, count_ref, query_ref, out_ref):
    row = iota((16, TOK), 0)
    col = iota((16, TOK), 1)
    hot = jnp.zeros((16, TOK), F32)
    for r in range(SLOTS):
        hot = jnp.where((row == r) & (col == index_ref[r]), 1.0, hot)
    rows = jnp.dot(hot.astype(BF), query_ref[...], preferred_element_type=F32)
    count = count_ref[0].astype(F32)
    place = iota((PAD, HD), 0)
    for h in range(HEADS):
        part = rows[:PAD, h * HD:(h + 1) * HD]
        out_ref[h] = jnp.where(place == SLOTS, count, part).astype(BF)


def choose(query, index, counts):
    return pl.pallas_call(
        choose_body,
        out_shape=jax.ShapeDtypeStruct((HEADS, PAD, HD), BF),
        in_specs=[SMEM, SMEM, VMEM],
        out_specs=VMEM,
        compiler_params=SMALL,
        name="choose",
    )(index, counts, query)


def split_body(per, key_ref, value_ref, out_ref):
    for h in range(per):
        out_ref[h, :TOK, :] = key_ref[:, h * HD:(h + 1) * HD]
        out_ref[h, TOK:, :] = value_ref[:, h * HD:(h + 1) * HD]


def split_heads(key, value):
    per = 8
    return pl.pallas_call(
        functools.partial(split_body, per),
        grid=(HEADS // per,),
        in_specs=[pl.BlockSpec((TOK, per * HD), lambda i: (0, i))] * 2,
        out_specs=pl.BlockSpec((per, 2 * TOK, HD), lambda i: (i, 0, 0)),
        out_shape=jax.ShapeDtypeStruct((HEADS, 2 * TOK, HD), BF),
        compiler_params=SMALL,
        name="split_heads",
    )(key, value)


def compact_body(rows_ref, out_ref, back_ref):
    n = HEADS * PAD
    rows = rows_ref[...].astype(F32).reshape(n, HD).astype(BF)
    down, across = iota((n, n), 0), iota((n, n), 1)
    pick = jnp.where(across == (down // PAD) * PAD + SLOTS, 1.0, 0.0).astype(BF)
    count_col = jnp.dot(pick, rows, preferred_element_type=F32)
    slot_col = iota((n, HD), 0) % PAD
    live_col = (slot_col.astype(F32) < count_col) & (slot_col < SLOTS)
    live_col = jnp.where(live_col, 1.0, 0.0)
    below = jnp.where(across < down, 1.0, 0.0).astype(BF)
    pos_col = jnp.dot(below, live_col.astype(BF), preferred_element_type=F32)
    pos_col = jnp.concatenate([pos_col, pos_col], 1)
    live_two = jnp.concatenate([live_col, live_col], 1)
    back_ref[...] = jnp.where(pos_col == across.astype(F32), live_two, 0.0).astype(BF)
    first = jnp.where(iota((16, HD), 1) == 0, 1.0, 0.0).astype(BF)
    live_row = lax.dot_general(first, live_col.astype(BF), NT, preferred_element_type=F32)
    above = jnp.where(down < across, 1.0, 0.0).astype(BF)
    pos_row = jnp.dot(live_row.astype(BF), above, preferred_element_type=F32)
    pos_row = jnp.broadcast_to(pos_row[:1], (n, n))
    live_row = jnp.broadcast_to(live_row[:1], (n, n))
    move = jnp.where(pos_row == down.astype(F32), live_row, 0.0).astype(BF)
    moved = jnp.dot(move, rows, preferred_element_type=F32)
    out_ref[:ROWS] = moved[:ROWS].astype(BF)
    total = jnp.sum(live_col, axis=0, keepdims=True)
    out_ref[ROWS:] = jnp.broadcast_to(total, (TAIL, HD)).astype(BF)


def compact(rows):
    n = HEADS * PAD
    return pl.pallas_call(
        compact_body,
        out_shape=(jax.ShapeDtypeStruct((MSG, HD), BF), jax.ShapeDtypeStruct((n, n), BF)),
        in_specs=[VMEM],
        out_specs=(VMEM, VMEM),
        compiler_params=SMALL,
        name="compact",
    )(rows)


def tail_of(first, second):
    place = iota((TAIL, HD), 0)
    tile = jnp.zeros((TAIL, HD), F32)
    for half, lanes in enumerate((first, second)):
        rest = lanes
        for term in range(3):
            piece = rest.astype(BF).astype(F32)
            rest = rest - piece
            tile = jnp.where(place == 2 * term + half, piece, tile)
    return tile.astype(BF)


def lanes_of(tail):
    tail = tail.astype(F32)
    return tail[0:2] + tail[2:4] + tail[4:6]


def column_to_lanes(column):
    n = column.shape[0]
    full = jnp.broadcast_to(column, (n, HD))
    out = []
    for at in (0, HD):
        size = min(HD, n - at)
        if size <= 0:
            out.append(jnp.zeros((1, HD), F32))
            continue
        diag = iota((size, HD), 0) == iota((size, HD), 1)
        out.append(jnp.sum(jnp.where(diag, full[at:at + size], 0.0), axis=0, keepdims=True))
    return out


def lanes_to_column(lanes, rows):
    out = []
    for half, size in enumerate((min(rows, HD), rows - HD)):
        if size <= 0:
            continue
        diag = iota((size, HD), 0) == iota((size, HD), 1)
        full = jnp.broadcast_to(lanes[half:half + 1], (size, HD))
        out.append(jnp.sum(jnp.where(diag, full, 0.0), axis=1, keepdims=True))
    return jnp.concatenate(out, 0)


def attend_rows(group, rows, query_ref, kv_ref, out_ref):
    size = group * rows
    query = query_ref[:, 0, :rows, :].reshape(size, HD)
    per = CHUNK // TOK
    top = mixed = total = None
    for j in range(KEYS // CHUNK):
        keys = kv_ref[j * per:(j + 1) * per, :TOK, :].reshape(CHUNK, HD)
        values = kv_ref[j * per:(j + 1) * per, TOK:, :].reshape(CHUNK, HD)
        scores = lax.dot_general(query, keys, NT, preferred_element_type=F32)
        high = scores[:, :HD]
        for t in range(1, per):
            high = jnp.maximum(high, scores[:, t * HD:(t + 1) * HD])
        high = jnp.broadcast_to(jnp.max(high, axis=1, keepdims=True) * SCALE, (size, HD))
        peak = high if top is None else jnp.maximum(top, high)
        weights, part_total = [], None
        for t in range(per):
            power = jnp.exp2(scores[:, t * HD:(t + 1) * HD] * SCALE - peak)
            part_total = power if part_total is None else part_total + power
            weights.append(power.astype(BF))
        part = jnp.dot(jnp.concatenate(weights, 1), values, preferred_element_type=F32)
        if top is None:
            mixed, total = part, part_total
        else:
            fade = jnp.exp2(top - peak)
            mixed = mixed * fade + part
            total = total * fade + part_total
        top = peak
    total = jnp.sum(total, axis=1, keepdims=True)
    out_ref[:, :rows, :] = (mixed / total).astype(BF).reshape(group, rows, HD)
    level = top[:, :1] + jnp.log2(total)
    for g in range(group):
        out_ref[g, rows:, :] = tail_of(*column_to_lanes(level[g * rows:(g + 1) * rows]))


def attend_body(group, rows, side_ref, query_ref, kv_ref, out_ref):
    attend_rows(group, rows, query_ref, kv_ref, out_ref)


def attend(rows, side, query, kv):
    group = 8 if rows == TIERS[0] else 4
    work = NZO * rows * KEYS * HD * 4
    return pl.pallas_call(
        functools.partial(attend_body, group, rows),
        grid_spec=pltpu.PrefetchScalarGridSpec(
            num_scalar_prefetch=1,
            grid=(NZO // group,),
            in_specs=[
                pl.BlockSpec((group, 1, MSG, HD), lambda i, side: (i, side[0], 0, 0)),
                pl.BlockSpec((HEADS, 2 * TOK, HD), lambda i, side: (0, 0, 0)),
            ],
            out_specs=pl.BlockSpec((group, rows + TAIL, HD), lambda i, side: (i, 0, 0)),
        ),
        out_shape=jax.ShapeDtypeStruct((NZO, rows + TAIL, HD), BF),
        compiler_params=pltpu.CompilerParams(vmem_limit_bytes=40 * 2**20),
        cost_estimate=pl.CostEstimate(
            flops=2 * work, bytes_accessed=6 * 2**20, transcendentals=NZO * rows * KEYS
        ),
        name="attend",
    )(side, query, kv)


def pair_body(group, rows, own_ref, other_ref, out_ref):
    for g in range(group):
        a, b = lanes_of(own_ref[g, rows:, :]), lanes_of(other_ref[g, rows:, :])
        peak = jnp.maximum(a, b)
        wa, wb = jnp.exp2(a - peak), jnp.exp2(b - peak)
        both = wa + wb
        level = peak + jnp.log2(both)
        ca, cb = lanes_to_column(wa / both, rows), lanes_to_column(wb / both, rows)
        out_ref[g, :rows, :] = (
            own_ref[g, :rows, :].astype(F32) * ca + other_ref[g, :rows, :].astype(F32) * cb
        ).astype(BF)
        out_ref[g, rows:, :] = tail_of(level[0:1], level[1:2])


def merge_pair(own, other):
    group = 4
    msg = own.shape[1]
    spec = pl.BlockSpec((group, msg, HD), lambda i: (i, 0, 0))
    return pl.pallas_call(
        functools.partial(pair_body, group, msg - TAIL),
        grid=(NZO // group,),
        in_specs=[spec, spec],
        out_specs=spec,
        out_shape=jax.ShapeDtypeStruct((NZO, msg, HD), BF),
        compiler_params=SMALL,
        name="merge_pair",
    )(own, other)


def finish_body(rows, parts_ref, live_ref, back_ref, out_ref):
    levels = [lanes_of(parts_ref[i, rows:, :]) for i in range(NZO)]
    peak = functools.reduce(jnp.maximum, levels)
    weights = [jnp.exp2(level - peak) for level in levels]
    both = functools.reduce(jnp.add, weights)
    mixed = None
    for i in range(NZO):
        column = lanes_to_column(weights[i] / both, rows)
        part = parts_ref[i, :rows, :].astype(F32) * column
        mixed = part if mixed is None else mixed + part
    count = live_ref[ROWS:, :].astype(F32)[:1]
    alive = iota((rows, HD), 0).astype(F32) < count
    mixed = jnp.where(alive, mixed, 0.0).astype(BF)
    placed = jnp.dot(back_ref[:, :rows], mixed, preferred_element_type=F32)
    out_ref[...] = placed.reshape(HEADS, PAD, HD).astype(BF)


def finish(parts, live, back):
    return pl.pallas_call(
        functools.partial(finish_body, parts.shape[1] - TAIL),
        out_shape=jax.ShapeDtypeStruct((HEADS, PAD, HD), BF),
        in_specs=[VMEM, VMEM, VMEM],
        out_specs=VMEM,
        compiler_params=SMALL,
        name="finish",
    )(parts, live, back)


def gate_body(count_ref, rows_ref, gate_ref, out_ref):
    alive = iota((PAD, HD), 0) < count_ref[0]
    for h in range(HEADS):
        gated = gate_ref[:, h * HD:(h + 1) * HD] * rows_ref[h].astype(F32)
        gated = jnp.where(alive, gated, 0.0)
        out_ref[:, h * HD:(h + 1) * HD] = gated[:SLOTS].astype(BF)


def apply_gate(counts, rows, gate):
    return pl.pallas_call(
        gate_body,
        out_shape=jax.ShapeDtypeStruct((SLOTS, HEADS * HD), BF),
        in_specs=[SMEM, VMEM, VMEM],
        out_specs=VMEM,
        compiler_params=SMALL,
        name="apply_gate",
    )(counts, rows, gate)


def after(value, token):
    return lax.optimization_barrier((value, token))[0]


def swap(x, axes):
    return lax.all_to_all(x, axes, split_axis=0, concat_axis=0, tiled=True)


def late(size, side, rows, kv, live, back):
    away = attend(size, 1 - side, rows, kv)
    arrived = lax.ppermute(away, "zi", [(0, 1), (1, 0)])
    own = attend(size, side, rows, kv)
    merged = merge_pair(own, arrived)
    parts = swap(merged, "zo")
    return finish(parts, live, back)


def local(query, key, value, index, counts, timestep, gate_table):
    side = lax.axis_index("zi").astype(jnp.int32).reshape(1)
    mine = choose(query, index, counts)
    kv = split_heads(key, value)
    plane_rows = swap(mine, PLANE)
    kv = swap(after(kv, plane_rows), PLANE)
    live, back = compact(plane_rows)
    rows = lax.all_gather(live, ("zo", "zi"), axis=0, tiled=False)
    rows = rows.reshape(NZO, 2, MSG, HD)
    most = jnp.max(rows[:, :, ROWS, 0].astype(F32))
    tier = sum((most > limit).astype(jnp.int32) for limit in TIERS[:-1])
    sent = lax.switch(tier, [functools.partial(late, n) for n in TIERS], side, rows, kv, live, back)
    heads = swap(sent, PLANE)
    gate = lax.dynamic_slice_in_dim(gate_table, timestep[0], 1, 0)
    return apply_gate(counts, heads, gate)


def solution(mesh):
    blk = mesh.shape["blk"]
    inner = Mesh(mesh.devices.reshape(NZO, 2, 2, blk), ("zo", "zi", "c", "blk"))
    every = ("zo", "zi", "c", "blk")
    in_specs = (
        P(every, None),
        P(every, None),
        P(every, None),
        P(every),
        P(every),
        P(),
        P(),
    )
    return jax.shard_map(
        local, mesh=inner, in_specs=in_specs, out_specs=P(every, None), check_vma=False
    )
```

```python
import functools
import math

import jax
import jax.numpy as jnp
from jax import lax
from jax.experimental import pallas as pl
from jax.experimental.pallas import tpu as pltpu
from jax.sharding import Mesh, PartitionSpec as P

HD = 128
HEADS = 32
TOK = 128
SLOTS = 6
PAD = 8
CHIPS_Z = 16
NZO = 8
ROWS = HEADS * SLOTS
TAIL = 16
TIERS = (128, 144, ROWS)
FIRST = TIERS[1]
DEAD = 64.0
SCALE = math.log2(math.e) / math.sqrt(HD)
KEYS = HEADS * TOK
CHUNK = 1024
BF = jnp.bfloat16
F32 = jnp.float32
NT = (((1,), (1,)), ((), ()))
PLANE = ("c", "blk")
SMALL = pltpu.CompilerParams(vmem_limit_bytes=12 * 2**20)
VMEM = pl.BlockSpec(memory_space=pltpu.VMEM)
SMEM = pl.BlockSpec(memory_space=pltpu.SMEM)


def iota(shape, dim):
    return lax.broadcasted_iota(jnp.int32, shape, dim)


def choose_body(index_ref, count_ref, query_ref, out_ref):
    row = iota((16, TOK), 0)
    col = iota((16, TOK), 1)
    hot = jnp.zeros((16, TOK), F32)
    for r in range(SLOTS):
        hot = jnp.where((row == r) & (col == index_ref[r]), 1.0, hot)
    rows = jnp.dot(hot.astype(BF), query_ref[...], preferred_element_type=F32)
    count = count_ref[0].astype(F32)
    place = iota((PAD, HD), 0)
    for h in range(HEADS):
        part = rows[:PAD, h * HD:(h + 1) * HD]
        out_ref[h] = jnp.where(place == SLOTS, count, part).astype(BF)


def choose(query, index, counts):
    return pl.pallas_call(
        choose_body,
        out_shape=jax.ShapeDtypeStruct((HEADS, PAD, HD), BF),
        in_specs=[SMEM, SMEM, VMEM],
        out_specs=VMEM,
        name="choose",
    )(index, counts, query)


def split_body(per, key_ref, value_ref, out_ref):
    for h in range(per):
        out_ref[h, :TOK, :] = key_ref[:, h * HD:(h + 1) * HD]
        out_ref[h, TOK:, :] = value_ref[:, h * HD:(h + 1) * HD]


def split_heads(key, value):
    per = 8
    return pl.pallas_call(
        functools.partial(split_body, per),
        grid=(HEADS // per,),
        in_specs=[pl.BlockSpec((TOK, per * HD), lambda i: (0, i))] * 2,
        out_specs=pl.BlockSpec((per, 2 * TOK, HD), lambda i: (i, 0, 0)),
        out_shape=jax.ShapeDtypeStruct((HEADS, 2 * TOK, HD), BF),
        name="split_heads",
    )(key, value)


def compact_body(rows_ref, out_ref, back_ref):
    n = HEADS * PAD
    rows = rows_ref[...].astype(F32).reshape(n, HD).astype(BF)
    down, across = iota((n, n), 0), iota((n, n), 1)
    pick = jnp.where(across == (down // PAD) * PAD + SLOTS, 1.0, 0.0).astype(BF)
    count_col = jnp.dot(pick, rows, preferred_element_type=F32)
    slot_col = iota((n, HD), 0) % PAD
    live_col = (slot_col.astype(F32) < count_col) & (slot_col < SLOTS)
    live_col = jnp.where(live_col, 1.0, 0.0)
    below = jnp.where(across < down, 1.0, 0.0).astype(BF)
    pos_col = jnp.dot(below, live_col.astype(BF), preferred_element_type=F32)
    pos_col = jnp.concatenate([pos_col, pos_col], 1)
    live_two = jnp.concatenate([live_col, live_col], 1)
    back_ref[...] = jnp.where(pos_col == across.astype(F32), live_two, 0.0).astype(BF)
    first = jnp.where(iota((16, HD), 1) == 0, 1.0, 0.0).astype(BF)
    live_row = lax.dot_general(first, live_col.astype(BF), NT, preferred_element_type=F32)
    above = jnp.where(down < across, 1.0, 0.0).astype(BF)
    pos_row = jnp.dot(live_row.astype(BF), above, preferred_element_type=F32)
    pos_row = jnp.broadcast_to(pos_row[:1], (n, n))
    live_row = jnp.broadcast_to(live_row[:1], (n, n))
    move = jnp.where(pos_row == down.astype(F32), live_row, 0.0).astype(BF)
    moved = jnp.dot(move, rows, preferred_element_type=F32)
    total = jnp.sum(live_col, axis=0, keepdims=True)
    alive = iota((ROWS, HD), 0).astype(F32) < total
    out_ref[...] = jnp.where(alive, moved[:ROWS], DEAD).astype(BF)


def compact(rows):
    n = HEADS * PAD
    return pl.pallas_call(
        compact_body,
        out_shape=(jax.ShapeDtypeStruct((ROWS, HD), BF), jax.ShapeDtypeStruct((n, n), BF)),
        in_specs=[VMEM],
        out_specs=(VMEM, VMEM),
        compiler_params=SMALL,
        name="compact",
    )(rows)


def tail_of(first, second):
    place = iota((TAIL, HD), 0)
    tile = jnp.zeros((TAIL, HD), F32)
    for half, lanes in enumerate((first, second)):
        rest = lanes
        for term in range(3):
            piece = rest.astype(BF).astype(F32)
            rest = rest - piece
            tile = jnp.where(place == 2 * term + half, piece, tile)
    return tile.astype(BF)


def lanes_of(tail):
    tail = tail.astype(F32)
    return tail[0:2] + tail[2:4] + tail[4:6]


def column_to_lanes(column):
    n = column.shape[0]
    full = jnp.broadcast_to(column, (n, HD))
    out = []
    for at in (0, HD):
        size = min(HD, n - at)
        if size <= 0:
            out.append(jnp.zeros((1, HD), F32))
            continue
        diag = iota((size, HD), 0) == iota((size, HD), 1)
        out.append(jnp.sum(jnp.where(diag, full[at:at + size], 0.0), axis=0, keepdims=True))
    return out


def lanes_to_column(lanes, rows):
    out = []
    for half, size in enumerate((min(rows, HD), rows - HD)):
        if size <= 0:
            continue
        diag = iota((size, HD), 0) == iota((size, HD), 1)
        full = jnp.broadcast_to(lanes[half:half + 1], (size, HD))
        out.append(jnp.sum(jnp.where(diag, full, 0.0), axis=1, keepdims=True))
    return jnp.concatenate(out, 0)


def attend_rows(rows, side, query_ref, kv_ref, out_ref, copies=()):
    size = NZO * rows
    query = query_ref[:, side, :rows, :].reshape(size, HD)
    per = CHUNK // TOK
    top = mixed = total = None
    for j in range(KEYS // CHUNK):
        if j < len(copies):
            copies[j].wait()
        keys = kv_ref[j * per:(j + 1) * per, :TOK, :].reshape(CHUNK, HD)
        values = kv_ref[j * per:(j + 1) * per, TOK:, :].reshape(CHUNK, HD)
        scores = lax.dot_general(query, keys, NT, preferred_element_type=F32)
        high = scores[:, :HD]
        for t in range(1, per):
            high = jnp.maximum(high, scores[:, t * HD:(t + 1) * HD])
        high = jnp.broadcast_to(jnp.max(high, axis=1, keepdims=True) * SCALE, (size, HD))
        peak = high if top is None else jnp.maximum(top, high)
        weights, part_total = [], None
        for t in range(per):
            power = jnp.exp2(scores[:, t * HD:(t + 1) * HD] * SCALE - peak)
            part_total = power if part_total is None else part_total + power
            weights.append(power.astype(BF))
        part = jnp.dot(jnp.concatenate(weights, 1), values, preferred_element_type=F32)
        if top is None:
            mixed, total = part, part_total
        else:
            fade = jnp.exp2(top - peak)
            mixed = mixed * fade + part
            total = total * fade + part_total
        top = peak
    total = jnp.sum(total, axis=1, keepdims=True)
    out_ref[:, :rows, :] = (mixed / total).astype(BF).reshape(NZO, rows, HD)
    level = top[:, :1] + jnp.log2(total)
    for g in range(NZO):
        out_ref[g, rows:, :] = tail_of(*column_to_lanes(level[g * rows:(g + 1) * rows]))


def load_and_attend_body(rows, side_ref, query_ref, far_ref, out_ref, kv_ref, sems):
    per = CHUNK // TOK
    copies = []
    for i, (at, size) in enumerate(((0, per), (per, HEADS - per))):
        here = pl.ds(at, size)
        copies.append(pltpu.make_async_copy(far_ref.at[here], kv_ref.at[here], sems.at[i]))
        copies[-1].start()
    attend_rows(rows, side_ref[0], query_ref, kv_ref, out_ref, copies)


def attend_body(rows, side_ref, query_ref, kv_ref, out_ref):
    attend_rows(rows, side_ref[0], query_ref, kv_ref, out_ref)


def attend_options(rows):
    return dict(
        compiler_params=pltpu.CompilerParams(vmem_limit_bytes=32 * 2**20),
        cost_estimate=pl.CostEstimate(
            flops=NZO * rows * KEYS * HD * 8,
            bytes_accessed=6 * 2**20,
            transcendentals=NZO * rows * KEYS,
        ),
    )


def load_and_attend(rows, side, query, kv):
    return pl.pallas_call(
        functools.partial(load_and_attend_body, rows),
        out_shape=(
            jax.ShapeDtypeStruct((NZO, rows + TAIL, HD), BF),
            jax.ShapeDtypeStruct(kv.shape, BF),
        ),
        in_specs=[SMEM, VMEM, pl.BlockSpec(memory_space=pl.ANY)],
        out_specs=(VMEM, VMEM),
        scratch_shapes=[pltpu.SemaphoreType.DMA((2,))],
        name="load_and_attend",
        **attend_options(rows),
    )(side, query, kv)


def attend(rows, side, query, kv):
    return pl.pallas_call(
        functools.partial(attend_body, rows),
        out_shape=jax.ShapeDtypeStruct((NZO, rows + TAIL, HD), BF),
        in_specs=[SMEM, VMEM, VMEM],
        out_specs=VMEM,
        name="attend",
        **attend_options(rows),
    )(side, query, kv)


def pair_body(group, rows, own_ref, other_ref, out_ref):
    for g in range(group):
        a, b = lanes_of(own_ref[g, rows:, :]), lanes_of(other_ref[g, rows:, :])
        peak = jnp.maximum(a, b)
        wa, wb = jnp.exp2(a - peak), jnp.exp2(b - peak)
        both = wa + wb
        level = peak + jnp.log2(both)
        ca, cb = lanes_to_column(wa / both, rows), lanes_to_column(wb / both, rows)
        out_ref[g, :rows, :] = (
            own_ref[g, :rows, :].astype(F32) * ca + other_ref[g, :rows, :].astype(F32) * cb
        ).astype(BF)
        out_ref[g, rows:, :] = tail_of(level[0:1], level[1:2])


def merge_pair(own, other):
    group = 4
    msg = own.shape[1]
    spec = pl.BlockSpec((group, msg, HD), lambda i: (i, 0, 0))
    return pl.pallas_call(
        functools.partial(pair_body, group, msg - TAIL),
        grid=(NZO // group,),
        in_specs=[spec, spec],
        out_specs=spec,
        out_shape=jax.ShapeDtypeStruct((NZO, msg, HD), BF),
        compiler_params=SMALL,
        name="merge_pair",
    )(own, other)


def finish_body(rows, parts_ref, live_ref, back_ref, out_ref):
    levels = [lanes_of(parts_ref[i, rows:, :]) for i in range(NZO)]
    peak = functools.reduce(jnp.maximum, levels)
    weights = [jnp.exp2(level - peak) for level in levels]
    both = functools.reduce(jnp.add, weights)
    mixed = None
    for i in range(NZO):
        column = lanes_to_column(weights[i] / both, rows)
        part = parts_ref[i, :rows, :].astype(F32) * column
        mixed = part if mixed is None else mixed + part
    alive = live_ref[:rows, :].astype(F32) < DEAD / 2
    mixed = jnp.where(alive, mixed, 0.0).astype(BF)
    placed = jnp.dot(back_ref[:, :rows], mixed, preferred_element_type=F32)
    out_ref[...] = placed.reshape(HEADS, PAD, HD).astype(BF)


def finish(parts, live, back):
    return pl.pallas_call(
        functools.partial(finish_body, parts.shape[1] - TAIL),
        out_shape=jax.ShapeDtypeStruct((HEADS, PAD, HD), BF),
        in_specs=[VMEM, VMEM, VMEM],
        out_specs=VMEM,
        compiler_params=SMALL,
        name="finish",
    )(parts, live, back)


def gate_body(count_ref, rows_ref, gate_ref, out_ref):
    alive = iota((PAD, HD), 0) < count_ref[0]
    for h in range(HEADS):
        gated = gate_ref[:, h * HD:(h + 1) * HD] * rows_ref[h].astype(F32)
        gated = jnp.where(alive, gated, 0.0)
        out_ref[:, h * HD:(h + 1) * HD] = gated[:SLOTS].astype(BF)


def apply_gate(counts, rows, gate):
    return pl.pallas_call(
        gate_body,
        out_shape=jax.ShapeDtypeStruct((SLOTS, HEADS * HD), BF),
        in_specs=[SMEM, VMEM, VMEM],
        out_specs=VMEM,
        compiler_params=SMALL,
        name="apply_gate",
    )(counts, rows, gate)


def after(value, token):
    return lax.optimization_barrier((value, token))[0]


def swap(x, axes):
    return lax.all_to_all(x, axes, split_axis=0, concat_axis=0, tiled=True)


def gather_z(x):
    return lax.all_gather(x, ("zo", "zi"), axis=0, tiled=False).reshape(NZO, 2, -1, HD)


def late(size, side, rows, kv, live, back):
    if size > FIRST:
        rows = jnp.concatenate([rows, gather_z(live[FIRST:])], axis=2)
    away, kv = load_and_attend(size, 1 - side, rows, kv)
    arrived = lax.ppermute(away, "zi", [(0, 1), (1, 0)])
    own = attend(size, side, rows, kv)
    merged = merge_pair(own, arrived)
    parts = swap(merged, "zo")
    return finish(parts, live, back)


def local(query, key, value, index, counts, timestep, gate_table):
    side = lax.axis_index("zi").astype(jnp.int32).reshape(1)
    mine = choose(query, index, counts)
    kv = split_heads(key, value)
    plane_rows = swap(mine, PLANE)
    kv = swap(after(kv, plane_rows), PLANE)
    live, back = compact(plane_rows)
    rows = gather_z(live[:FIRST])
    tail = rows[:, :, TIERS[0]:, 0]
    fullest = jnp.where(iota(tail.shape, 2) == FIRST - TIERS[0] - 1, 2, 1)
    tier = jnp.max(jnp.where(tail.astype(F32) < DEAD / 2, fullest, 0))
    sent = lax.switch(tier, [functools.partial(late, n) for n in TIERS], side, rows, kv, live, back)
    heads = swap(sent, PLANE)
    gate = lax.dynamic_slice_in_dim(gate_table, timestep[0], 1, 0)
    return apply_gate(counts, heads, gate)


def solution(mesh):
    blk = mesh.shape["blk"]
    inner = Mesh(mesh.devices.reshape(NZO, 2, 2, blk), ("zo", "zi", "c", "blk"))
    every = ("zo", "zi", "c", "blk")
    in_specs = (
        P(every, None),
        P(every, None),
        P(every, None),
        P(every),
        P(every),
        P(),
        P(),
    )
    return jax.shard_map(
        local, mesh=inner, in_specs=in_specs, out_specs=P(every, None), check_vma=False
    )
```

```python
import functools
import math

import jax
import jax.numpy as jnp
from jax import lax
from jax.experimental import pallas as pl
from jax.experimental.pallas import tpu as pltpu
from jax.sharding import Mesh, PartitionSpec as P

HD = 128
HEADS = 32
TOK = 128
SLOTS = 6
PAD = 8
CHIPS_Z = 16
NZO = 8
ROWS = HEADS * SLOTS
TAIL = 16
FIRST = 144
DEAD = 64.0
SCALE = math.log2(math.e) / math.sqrt(HD)
KEYS = HEADS * TOK
CHUNK = 1024
BF = jnp.bfloat16
F32 = jnp.float32
NT = (((1,), (1,)), ((), ()))
PLANE = ("c", "blk")
SMALL = pltpu.CompilerParams(vmem_limit_bytes=12 * 2**20)
VMEM = pl.BlockSpec(memory_space=pltpu.VMEM)
SMEM = pl.BlockSpec(memory_space=pltpu.SMEM)


def iota(shape, dim):
    return lax.broadcasted_iota(jnp.int32, shape, dim)


def choose_body(index_ref, count_ref, query_ref, out_ref):
    row = iota((16, TOK), 0)
    col = iota((16, TOK), 1)
    hot = jnp.zeros((16, TOK), F32)
    for r in range(SLOTS):
        hot = jnp.where((row == r) & (col == index_ref[r]), 1.0, hot)
    rows = jnp.dot(hot.astype(BF), query_ref[...], preferred_element_type=F32)
    count = count_ref[0].astype(F32)
    place = iota((PAD, HD), 0)
    for h in range(HEADS):
        part = rows[:PAD, h * HD:(h + 1) * HD]
        out_ref[h] = jnp.where(place == SLOTS, count, part).astype(BF)


def choose(query, index, counts):
    return pl.pallas_call(
        choose_body,
        out_shape=jax.ShapeDtypeStruct((HEADS, PAD, HD), BF),
        in_specs=[SMEM, SMEM, VMEM],
        out_specs=VMEM,
        name="choose",
    )(index, counts, query)


def split_body(per, key_ref, value_ref, out_ref):
    for h in range(per):
        out_ref[h, :TOK, :] = key_ref[:, h * HD:(h + 1) * HD]
        out_ref[h, TOK:, :] = value_ref[:, h * HD:(h + 1) * HD]


def split_heads(key, value):
    per = 8
    return pl.pallas_call(
        functools.partial(split_body, per),
        grid=(HEADS // per,),
        in_specs=[pl.BlockSpec((TOK, per * HD), lambda i: (0, i))] * 2,
        out_specs=pl.BlockSpec((per, 2 * TOK, HD), lambda i: (i, 0, 0)),
        out_shape=jax.ShapeDtypeStruct((HEADS, 2 * TOK, HD), BF),
        name="split_heads",
    )(key, value)


def compact_body(kept, rows_ref, out_ref, back_ref):
    n = HEADS * PAD
    rows = rows_ref[...].astype(F32).reshape(n, HD).astype(BF)
    down, across = iota((n, n), 0), iota((n, n), 1)
    pick = jnp.where(across == (down // PAD) * PAD + SLOTS, 1.0, 0.0).astype(BF)
    count_col = jnp.dot(pick, rows, preferred_element_type=F32)
    slot_col = iota((n, HD), 0) % PAD
    live_col = (slot_col.astype(F32) < count_col) & (slot_col < SLOTS)
    live_col = jnp.where(live_col, 1.0, 0.0)
    below = jnp.where(across < down, 1.0, 0.0).astype(BF)
    pos_col = jnp.dot(below, live_col.astype(BF), preferred_element_type=F32)
    pos_col = jnp.concatenate([pos_col, pos_col], 1)
    live_two = jnp.concatenate([live_col, live_col], 1)
    back_ref[...] = jnp.where(pos_col == across.astype(F32), live_two, 0.0).astype(BF)
    first = jnp.where(iota((16, HD), 1) == 0, 1.0, 0.0).astype(BF)
    live_row = lax.dot_general(first, live_col.astype(BF), NT, preferred_element_type=F32)
    above = jnp.where(down < across, 1.0, 0.0).astype(BF)
    pos_row = jnp.dot(live_row.astype(BF), above, preferred_element_type=F32)
    pos_row = jnp.broadcast_to(pos_row[:1], (n, n))
    live_row = jnp.broadcast_to(live_row[:1], (n, n))
    move = jnp.where(pos_row == down.astype(F32), live_row, 0.0).astype(BF)
    moved = jnp.dot(move, rows, preferred_element_type=F32)
    total = jnp.sum(live_col, axis=0, keepdims=True)
    alive = iota((kept, HD), 0).astype(F32) < total
    out_ref[...] = jnp.where(alive, moved[:kept], DEAD).astype(BF)


def compact(kept, rows):
    n = HEADS * PAD
    return pl.pallas_call(
        functools.partial(compact_body, kept),
        out_shape=(jax.ShapeDtypeStruct((kept, HD), BF), jax.ShapeDtypeStruct((n, n), BF)),
        in_specs=[VMEM],
        out_specs=(VMEM, VMEM),
        compiler_params=SMALL,
        name="compact",
    )(rows)


def tail_of(first, second):
    place = iota((TAIL, HD), 0)
    tile = jnp.zeros((TAIL, HD), F32)
    for half, lanes in enumerate((first, second)):
        rest = lanes
        for term in range(3):
            piece = rest.astype(BF).astype(F32)
            rest = rest - piece
            tile = jnp.where(place == 2 * term + half, piece, tile)
    return tile.astype(BF)


def lanes_of(tail):
    tail = tail.astype(F32)
    return tail[0:2] + tail[2:4] + tail[4:6]


def column_to_lanes(column):
    n = column.shape[0]
    full = jnp.broadcast_to(column, (n, HD))
    out = []
    for at in (0, HD):
        size = min(HD, n - at)
        if size <= 0:
            out.append(jnp.zeros((1, HD), F32))
            continue
        diag = iota((size, HD), 0) == iota((size, HD), 1)
        out.append(jnp.sum(jnp.where(diag, full[at:at + size], 0.0), axis=0, keepdims=True))
    return out


def lanes_to_column(lanes, rows):
    out = []
    for half, size in enumerate((min(rows, HD), rows - HD)):
        if size <= 0:
            continue
        diag = iota((size, HD), 0) == iota((size, HD), 1)
        full = jnp.broadcast_to(lanes[half:half + 1], (size, HD))
        out.append(jnp.sum(jnp.where(diag, full, 0.0), axis=1, keepdims=True))
    return jnp.concatenate(out, 0)


def attend_body(side_ref, query_ref, kv_ref, out_ref):
    rows = query_ref.shape[2]
    size = NZO * rows
    query = query_ref[:, side_ref[0], :, :].reshape(size, HD)
    per = CHUNK // TOK
    top = mixed = total = None
    for j in range(KEYS // CHUNK):
        keys = kv_ref[j * per:(j + 1) * per, :TOK, :].reshape(CHUNK, HD)
        values = kv_ref[j * per:(j + 1) * per, TOK:, :].reshape(CHUNK, HD)
        scores = lax.dot_general(query, keys, NT, preferred_element_type=F32)
        high = scores[:, :HD]
        for t in range(1, per):
            high = jnp.maximum(high, scores[:, t * HD:(t + 1) * HD])
        high = jnp.broadcast_to(jnp.max(high, axis=1, keepdims=True) * SCALE, (size, HD))
        peak = high if top is None else jnp.maximum(top, high)
        weights, part_total = [], None
        for t in range(per):
            power = jnp.exp2(scores[:, t * HD:(t + 1) * HD] * SCALE - peak)
            part_total = power if part_total is None else part_total + power
            weights.append(power.astype(BF))
        part = jnp.dot(jnp.concatenate(weights, 1), values, preferred_element_type=F32)
        if top is None:
            mixed, total = part, part_total
        else:
            fade = jnp.exp2(top - peak)
            mixed = mixed * fade + part
            total = total * fade + part_total
        top = peak
    total = jnp.sum(total, axis=1, keepdims=True)
    out_ref[:, :rows, :] = (mixed / total).astype(BF).reshape(NZO, rows, HD)
    level = top[:, :1] + jnp.log2(total)
    for g in range(NZO):
        out_ref[g, rows:, :] = tail_of(*column_to_lanes(level[g * rows:(g + 1) * rows]))


def attend(side, query, kv):
    rows = query.shape[2]
    return pl.pallas_call(
        attend_body,
        out_shape=jax.ShapeDtypeStruct((NZO, rows + TAIL, HD), BF),
        in_specs=[SMEM, VMEM, VMEM],
        out_specs=VMEM,
        compiler_params=pltpu.CompilerParams(vmem_limit_bytes=32 * 2**20),
        cost_estimate=pl.CostEstimate(
            flops=NZO * rows * KEYS * HD * 8,
            bytes_accessed=6 * 2**20,
            transcendentals=NZO * rows * KEYS,
        ),
        name="attend",
    )(side, query, kv)


def pair_body(group, rows, own_ref, other_ref, out_ref):
    for g in range(group):
        a, b = lanes_of(own_ref[g, rows:, :]), lanes_of(other_ref[g, rows:, :])
        peak = jnp.maximum(a, b)
        wa, wb = jnp.exp2(a - peak), jnp.exp2(b - peak)
        both = wa + wb
        level = peak + jnp.log2(both)
        ca, cb = lanes_to_column(wa / both, rows), lanes_to_column(wb / both, rows)
        out_ref[g, :rows, :] = (
            own_ref[g, :rows, :].astype(F32) * ca + other_ref[g, :rows, :].astype(F32) * cb
        ).astype(BF)
        out_ref[g, rows:, :] = tail_of(level[0:1], level[1:2])


def merge_pair(own, other):
    group = 4
    msg = own.shape[1]
    spec = pl.BlockSpec((group, msg, HD), lambda i: (i, 0, 0))
    return pl.pallas_call(
        functools.partial(pair_body, group, msg - TAIL),
        grid=(NZO // group,),
        in_specs=[spec, spec],
        out_specs=spec,
        out_shape=jax.ShapeDtypeStruct((NZO, msg, HD), BF),
        compiler_params=SMALL,
        name="merge_pair",
    )(own, other)


def finish_body(rows, parts_ref, live_ref, back_ref, out_ref):
    levels = [lanes_of(parts_ref[i, rows:, :]) for i in range(NZO)]
    peak = functools.reduce(jnp.maximum, levels)
    weights = [jnp.exp2(level - peak) for level in levels]
    both = functools.reduce(jnp.add, weights)
    mixed = None
    for i in range(NZO):
        column = lanes_to_column(weights[i] / both, rows)
        part = parts_ref[i, :rows, :].astype(F32) * column
        mixed = part if mixed is None else mixed + part
    alive = live_ref[...].astype(F32) < DEAD / 2
    mixed = jnp.where(alive, mixed, 0.0).astype(BF)
    placed = jnp.dot(back_ref[:, :rows], mixed, preferred_element_type=F32)
    out_ref[...] = placed.reshape(HEADS, PAD, HD).astype(BF)


def finish(parts, live, back):
    return pl.pallas_call(
        functools.partial(finish_body, parts.shape[1] - TAIL),
        out_shape=jax.ShapeDtypeStruct((HEADS, PAD, HD), BF),
        in_specs=[VMEM, VMEM, VMEM],
        out_specs=VMEM,
        compiler_params=SMALL,
        name="finish",
    )(parts, live, back)


def gate_body(count_ref, rows_ref, gate_ref, out_ref):
    alive = iota((PAD, HD), 0) < count_ref[0]
    for h in range(HEADS):
        gated = gate_ref[:, h * HD:(h + 1) * HD] * rows_ref[h].astype(F32)
        gated = jnp.where(alive, gated, 0.0)
        out_ref[:, h * HD:(h + 1) * HD] = gated[:SLOTS].astype(BF)


def apply_gate(counts, rows, gate):
    return pl.pallas_call(
        gate_body,
        out_shape=jax.ShapeDtypeStruct((SLOTS, HEADS * HD), BF),
        in_specs=[SMEM, VMEM, VMEM],
        out_specs=VMEM,
        compiler_params=SMALL,
        name="apply_gate",
    )(counts, rows, gate)


def after(value, token):
    return lax.optimization_barrier((value, token))[0]


def swap(x, axes):
    return lax.all_to_all(x, axes, split_axis=0, concat_axis=0, tiled=True)


def whole(kept, query, key, value, index, counts, gate):
    side = lax.axis_index("zi").astype(jnp.int32).reshape(1)
    mine = choose(query, index, counts)
    kv = split_heads(key, value)
    plane_rows = swap(mine, PLANE)
    kv = swap(after(kv, plane_rows), PLANE)
    live, back = compact(kept, plane_rows)
    rows = lax.all_gather(live, ("zo", "zi"), axis=0, tiled=False).reshape(NZO, 2, kept, HD)
    away = attend(1 - side, rows, kv)
    arrived = lax.ppermute(away, "zi", [(0, 1), (1, 0)])
    own = attend(side, rows, kv)
    merged = merge_pair(own, arrived)
    parts = swap(merged, "zo")
    heads = swap(finish(parts, live, back), PLANE)
    return apply_gate(counts, heads, gate), rows


def local(query, key, value, index, counts, timestep, gate_table):
    gate = lax.dynamic_slice_in_dim(gate_table, timestep[0], 1, 0)
    usual, rows = whole(FIRST, query, key, value, index, counts, gate)
    full = jnp.min(rows[:, :, FIRST - 1, 0].astype(F32)) < DEAD / 2
    full, usual = lax.optimization_barrier((full, usual))

    def again(usual, *args):
        return whole(ROWS, *args)[0]

    def keep(usual, *args):
        return usual

    return lax.cond(full, again, keep, usual, query, key, value, index, counts, gate)


def solution(mesh):
    blk = mesh.shape["blk"]
    inner = Mesh(mesh.devices.reshape(NZO, 2, 2, blk), ("zo", "zi", "c", "blk"))
    every = ("zo", "zi", "c", "blk")
    in_specs = (
        P(every, None),
        P(every, None),
        P(every, None),
        P(every),
        P(every),
        P(),
        P(),
    )
    return jax.shard_map(
        local, mesh=inner, in_specs=in_specs, out_specs=P(every, None), check_vma=False
    )
```

```python
import functools
import math

import jax
import jax.numpy as jnp
from jax import lax
from jax.experimental import pallas as pl
from jax.experimental.pallas import tpu as pltpu
from jax.sharding import Mesh, PartitionSpec as P

HD = 128
HEADS = 32
TOK = 128
SLOTS = 6
PAD = 8
CHIPS_Z = 16
NZO = 8
ROWS = HEADS * SLOTS
TAIL = 16
FIRST = 144
DEAD = 64.0
SCALE = math.log2(math.e) / math.sqrt(HD)
KEYS = HEADS * TOK
CHUNK = 1024
BF = jnp.bfloat16
F32 = jnp.float32
NT = (((1,), (1,)), ((), ()))
PLANE = ("c", "blk")
SMALL = pltpu.CompilerParams(vmem_limit_bytes=12 * 2**20)
VMEM = pl.BlockSpec(memory_space=pltpu.VMEM)
SMEM = pl.BlockSpec(memory_space=pltpu.SMEM)


def iota(shape, dim):
    return lax.broadcasted_iota(jnp.int32, shape, dim)


def choose_body(index_ref, count_ref, query_ref, out_ref):
    row = iota((16, TOK), 0)
    col = iota((16, TOK), 1)
    hot = jnp.zeros((16, TOK), F32)
    for r in range(SLOTS):
        hot = jnp.where((row == r) & (col == index_ref[r]), 1.0, hot)
    rows = jnp.dot(hot.astype(BF), query_ref[...], preferred_element_type=F32)
    count = count_ref[0].astype(F32)
    place = iota((PAD, HD), 0)
    for h in range(HEADS):
        part = rows[:PAD, h * HD:(h + 1) * HD]
        out_ref[h] = jnp.where(place == SLOTS, count, part).astype(BF)


def choose(query, index, counts):
    return pl.pallas_call(
        choose_body,
        out_shape=jax.ShapeDtypeStruct((HEADS, PAD, HD), BF),
        in_specs=[SMEM, SMEM, VMEM],
        out_specs=VMEM,
        name="choose",
    )(index, counts, query)


def split_body(per, key_ref, value_ref, out_ref):
    for h in range(per):
        out_ref[h, :TOK, :] = key_ref[:, h * HD:(h + 1) * HD]
        out_ref[h, TOK:, :] = value_ref[:, h * HD:(h + 1) * HD]


def split_heads(key, value):
    per = 8
    return pl.pallas_call(
        functools.partial(split_body, per),
        grid=(HEADS // per,),
        in_specs=[pl.BlockSpec((TOK, per * HD), lambda i: (0, i))] * 2,
        out_specs=pl.BlockSpec((per, 2 * TOK, HD), lambda i: (i, 0, 0)),
        out_shape=jax.ShapeDtypeStruct((HEADS, 2 * TOK, HD), BF),
        name="split_heads",
    )(key, value)


def compact_body(kept, rows_ref, out_ref, back_ref):
    n = HEADS * PAD
    rows = rows_ref[...].astype(F32).reshape(n, HD).astype(BF)
    down, across = iota((n, n), 0), iota((n, n), 1)
    pick = jnp.where(across == (down // PAD) * PAD + SLOTS, 1.0, 0.0).astype(BF)
    count_col = jnp.dot(pick, rows, preferred_element_type=F32)
    slot_col = iota((n, HD), 0) % PAD
    live_col = (slot_col.astype(F32) < count_col) & (slot_col < SLOTS)
    live_col = jnp.where(live_col, 1.0, 0.0)
    below = jnp.where(across < down, 1.0, 0.0).astype(BF)
    pos_col = jnp.dot(below, live_col.astype(BF), preferred_element_type=F32)
    pos_col = jnp.concatenate([pos_col, pos_col], 1)
    live_two = jnp.concatenate([live_col, live_col], 1)
    back_ref[...] = jnp.where(pos_col == across.astype(F32), live_two, 0.0).astype(BF)
    first = jnp.where(iota((16, HD), 1) == 0, 1.0, 0.0).astype(BF)
    live_row = lax.dot_general(first, live_col.astype(BF), NT, preferred_element_type=F32)
    above = jnp.where(down < across, 1.0, 0.0).astype(BF)
    pos_row = jnp.dot(live_row.astype(BF), above, preferred_element_type=F32)
    pos_row = jnp.broadcast_to(pos_row[:1], (n, n))
    live_row = jnp.broadcast_to(live_row[:1], (n, n))
    move = jnp.where(pos_row == down.astype(F32), live_row, 0.0).astype(BF)
    moved = jnp.dot(move, rows, preferred_element_type=F32)
    total = jnp.sum(live_col, axis=0, keepdims=True)
    alive = iota((kept, HD), 0).astype(F32) < total
    out_ref[...] = jnp.where(alive, moved[:kept], DEAD).astype(BF)


def compact(kept, rows):
    n = HEADS * PAD
    return pl.pallas_call(
        functools.partial(compact_body, kept),
        out_shape=(jax.ShapeDtypeStruct((kept, HD), BF), jax.ShapeDtypeStruct((n, n), BF)),
        in_specs=[VMEM],
        out_specs=(VMEM, VMEM),
        compiler_params=SMALL,
        name="compact",
    )(rows)


def tail_of(first, second):
    place = iota((TAIL, HD), 0)
    tile = jnp.zeros((TAIL, HD), F32)
    for half, lanes in enumerate((first, second)):
        rest = lanes
        for term in range(3):
            piece = rest.astype(BF).astype(F32)
            rest = rest - piece
            tile = jnp.where(place == 2 * term + half, piece, tile)
    return tile.astype(BF)


def lanes_of(tail):
    tail = tail.astype(F32)
    return tail[0:2] + tail[2:4] + tail[4:6]


def column_to_lanes(column):
    n = column.shape[0]
    full = jnp.broadcast_to(column, (n, HD))
    out = []
    for at in (0, HD):
        size = min(HD, n - at)
        if size <= 0:
            out.append(jnp.zeros((1, HD), F32))
            continue
        diag = iota((size, HD), 0) == iota((size, HD), 1)
        out.append(jnp.sum(jnp.where(diag, full[at:at + size], 0.0), axis=0, keepdims=True))
    return out


def lanes_to_column(lanes, rows):
    out = []
    for half, size in enumerate((min(rows, HD), rows - HD)):
        if size <= 0:
            continue
        diag = iota((size, HD), 0) == iota((size, HD), 1)
        full = jnp.broadcast_to(lanes[half:half + 1], (size, HD))
        out.append(jnp.sum(jnp.where(diag, full, 0.0), axis=1, keepdims=True))
    return jnp.concatenate(out, 0)


def attend_body(side_ref, query_ref, kv_ref, out_ref):
    rows = query_ref.shape[2]
    size = NZO * rows
    query = query_ref[:, side_ref[0], :, :].reshape(size, HD)
    per = CHUNK // TOK
    top = mixed = total = None
    for j in range(KEYS // CHUNK):
        keys = kv_ref[j * per:(j + 1) * per, :TOK, :].reshape(CHUNK, HD)
        values = kv_ref[j * per:(j + 1) * per, TOK:, :].reshape(CHUNK, HD)
        scores = lax.dot_general(query, keys, NT, preferred_element_type=F32)
        high = scores[:, :HD]
        for t in range(1, per):
            high = jnp.maximum(high, scores[:, t * HD:(t + 1) * HD])
        high = jnp.broadcast_to(jnp.max(high, axis=1, keepdims=True) * SCALE, (size, HD))
        peak = high if top is None else jnp.maximum(top, high)
        weights, part_total = [], None
        for t in range(per):
            power = jnp.exp2(scores[:, t * HD:(t + 1) * HD] * SCALE - peak)
            part_total = power if part_total is None else part_total + power
            weights.append(power.astype(BF))
        part = jnp.dot(jnp.concatenate(weights, 1), values, preferred_element_type=F32)
        if top is None:
            mixed, total = part, part_total
        else:
            fade = jnp.exp2(top - peak)
            mixed = mixed * fade + part
            total = total * fade + part_total
        top = peak
    total = jnp.sum(total, axis=1, keepdims=True)
    out_ref[:, :rows, :] = (mixed / total).astype(BF).reshape(NZO, rows, HD)
    level = top[:, :1] + jnp.log2(total)
    for g in range(NZO):
        out_ref[g, rows:, :] = tail_of(*column_to_lanes(level[g * rows:(g + 1) * rows]))


def attend(side, query, kv):
    rows = query.shape[2]
    return pl.pallas_call(
        attend_body,
        out_shape=jax.ShapeDtypeStruct((NZO, rows + TAIL, HD), BF),
        in_specs=[SMEM, VMEM, VMEM],
        out_specs=VMEM,
        compiler_params=pltpu.CompilerParams(vmem_limit_bytes=32 * 2**20),
        cost_estimate=pl.CostEstimate(
            flops=NZO * rows * KEYS * HD * 8,
            bytes_accessed=6 * 2**20,
            transcendentals=NZO * rows * KEYS,
        ),
        name="attend",
    )(side, query, kv)


def pair_body(group, rows, own_ref, other_ref, out_ref):
    for g in range(group):
        a, b = lanes_of(own_ref[g, rows:, :]), lanes_of(other_ref[g, rows:, :])
        peak = jnp.maximum(a, b)
        wa, wb = jnp.exp2(a - peak), jnp.exp2(b - peak)
        both = wa + wb
        level = peak + jnp.log2(both)
        ca, cb = lanes_to_column(wa / both, rows), lanes_to_column(wb / both, rows)
        out_ref[g, :rows, :] = (
            own_ref[g, :rows, :].astype(F32) * ca + other_ref[g, :rows, :].astype(F32) * cb
        ).astype(BF)
        out_ref[g, rows:, :] = tail_of(level[0:1], level[1:2])


def merge_pair(own, other):
    return pl.pallas_call(
        functools.partial(pair_body, NZO, own.shape[1] - TAIL),
        out_shape=jax.ShapeDtypeStruct(own.shape, BF),
        in_specs=[VMEM, VMEM],
        out_specs=VMEM,
        compiler_params=SMALL,
        name="merge_pair",
    )(own, other)


def finish_body(rows, parts_ref, live_ref, back_ref, out_ref):
    levels = [lanes_of(parts_ref[i, rows:, :]) for i in range(NZO)]
    peak = functools.reduce(jnp.maximum, levels)
    weights = [jnp.exp2(level - peak) for level in levels]
    both = functools.reduce(jnp.add, weights)
    mixed = None
    for i in range(NZO):
        column = lanes_to_column(weights[i] / both, rows)
        part = parts_ref[i, :rows, :].astype(F32) * column
        mixed = part if mixed is None else mixed + part
    alive = live_ref[...].astype(F32) < DEAD / 2
    mixed = jnp.where(alive, mixed, 0.0).astype(BF)
    placed = jnp.dot(back_ref[:, :rows], mixed, preferred_element_type=F32)
    out_ref[...] = placed.reshape(HEADS, PAD, HD).astype(BF)


def finish(parts, live, back):
    return pl.pallas_call(
        functools.partial(finish_body, parts.shape[1] - TAIL),
        out_shape=jax.ShapeDtypeStruct((HEADS, PAD, HD), BF),
        in_specs=[VMEM, VMEM, VMEM],
        out_specs=VMEM,
        compiler_params=SMALL,
        name="finish",
    )(parts, live, back)


def gate_body(count_ref, rows_ref, gate_ref, out_ref):
    alive = iota((PAD, HD), 0) < count_ref[0]
    for h in range(HEADS):
        gated = gate_ref[:, h * HD:(h + 1) * HD] * rows_ref[h].astype(F32)
        gated = jnp.where(alive, gated, 0.0)
        out_ref[:, h * HD:(h + 1) * HD] = gated[:SLOTS].astype(BF)


def apply_gate(counts, rows, gate):
    return pl.pallas_call(
        gate_body,
        out_shape=jax.ShapeDtypeStruct((SLOTS, HEADS * HD), BF),
        in_specs=[SMEM, VMEM, VMEM],
        out_specs=VMEM,
        compiler_params=SMALL,
        name="apply_gate",
    )(counts, rows, gate)


def after(value, token):
    return lax.optimization_barrier((value, token))[0]


def swap(x, axes):
    return lax.all_to_all(x, axes, split_axis=0, concat_axis=0, tiled=True)


def whole(kept, query, key, value, index, counts):
    side = lax.axis_index("zi").astype(jnp.int32).reshape(1)
    mine = choose(query, index, counts)
    kv = split_heads(key, value)
    plane_rows = swap(mine, PLANE)
    kv = swap(after(kv, plane_rows), PLANE)
    live, back = compact(kept, plane_rows)
    rows = lax.all_gather(live, ("zo", "zi"), axis=0, tiled=False).reshape(NZO, 2, kept, HD)
    away = attend(1 - side, rows, kv)
    arrived = lax.ppermute(away, "zi", [(0, 1), (1, 0)])
    own = attend(side, rows, kv)
    merged = merge_pair(own, arrived)
    parts = swap(merged, "zo")
    return swap(finish(parts, live, back), PLANE), rows


def local(query, key, value, index, counts, timestep, gate_table):
    gate = lax.dynamic_slice_in_dim(gate_table, timestep[0], 1, 0)
    usual, rows = whole(FIRST, query, key, value, index, counts)
    full = jnp.min(rows[:, :, FIRST - 1, 0].astype(F32)) < DEAD / 2
    full, usual = lax.optimization_barrier((full, usual))

    def again(usual, *args):
        return whole(ROWS, *args)[0]

    def keep(usual, *args):
        return usual

    heads = lax.cond(full, again, keep, usual, query, key, value, index, counts)
    return apply_gate(counts, heads, gate)


def solution(mesh):
    blk = mesh.shape["blk"]
    inner = Mesh(mesh.devices.reshape(NZO, 2, 2, blk), ("zo", "zi", "c", "blk"))
    every = ("zo", "zi", "c", "blk")
    in_specs = (
        P(every, None),
        P(every, None),
        P(every, None),
        P(every),
        P(every),
        P(),
        P(),
    )
    return jax.shard_map(
        local, mesh=inner, in_specs=in_specs, out_specs=P(every, None), check_vma=False
    )
```
